32 devices in a mesh: segment: 4 (over y, x), blk: 8 (over z, core).
Axes of the slice: x: 2, y: 2, z: 4, core: 2. Of those that a mesh axis runs over, the one named last changes fastest.
Arguments:
- echoes: bfloat16 [4, 512, 128, 512], P('segment', 'blk'), may hold values from -6 to 6
- train_blocks: int32 [4, 256, 6], P('segment', 'blk'), may hold values from 0 to 15, as said below
- hard_bins: int32 [4, 256], P('segment', 'blk'), may hold values 0 or 1
- owner_map: int32 [256], replicated, may hold values from 0 to 255, each once
- code_phase: float32 [64], replicated, may hold values from -3.140625 to 3.140625
Outputs:
- returns: bfloat16 [4, 256, 512, 256], P('segment', 'blk')
The draws below stay inside these ranges and needn't reach their ends.
Inputs may be any that keep to these rules, and one draw needn't show every extreme that they name: `train_blocks`: each row lists 6 different training blocks.
All inputs are finite; a program needn't handle non-finite values. No bound on the sum of `hard_bins` on one device may be relied on, other than what follows from the above.
Results may differ from the reference program's by a relative error of at most 0.0086.
Values may be sent and summed in bfloat16 or wider, within the bound.
A program may use at most 128 MiB of HBM per device.

```python
import math
import jax
import jax.numpy as jnp
from jax import lax

CH = 128
PULSES = 256
BEAMS = 128
RB = 32
NTR = 6
NTR_EASY = 3
NS_STEPS = 12
CBLK = 128
CODE_LEN = 64
BINS = 256
INTERVALS = 4
RANGES = 512
NBLOCKS = 16


def draw_train_blocks(key, part):
    row_keys = jax.random.split(key, INTERVALS * BINS)

    def listing(row_key):
        return jax.random.permutation(row_key, NBLOCKS)[:NTR]
    listed = jax.vmap(listing)(row_keys)
    return listed.reshape(INTERVALS, BINS, NTR).astype(jnp.int32)


def with_ends(entries, rng, low, largest):
    shape = entries.shape
    place = [jax.random.randint(jax.random.fold_in(rng, axis), (), 0, shape[axis]) for axis in range(len(shape))]
    entries = entries.at[tuple(place)].set(low)
    longest = shape.index(max(shape))
    place[longest] = (place[longest] + 1) % shape[longest]
    return entries.at[tuple(place)].set(largest)


def block_scale(own_key, shape, pieces, least, top_value):
    def one(position, shards_of):
        draws = jax.random.uniform(jax.random.fold_in(jax.random.fold_in(own_key, 6), position), (shards_of,), jnp.float32, least / len(pieces), top_value / len(pieces))
        return jnp.repeat(jnp.exp(draws), shape[position] // shards_of).reshape((-1,) + (1,) * (len(shape) - position - 1))

    factor_of = one(*pieces[0])
    for cut in pieces[1:]:
        factor_of = factor_of * one(*cut)
    return factor_of


def scatter_about(key, shape, width, limit, pieces=(), held_as=jnp.bfloat16):
    result = jax.random.normal(key, shape, jnp.float32) * width
    if len(pieces) > 0:
        result = block_scale(key, shape, pieces, -0.22, 0.18) * result
    return jnp.clip(result, min=-limit, max=limit).astype(held_as)


def setup_inputs(seed: int = 0) -> dict:
    key_of = jax.random.split(jax.random.key(seed), 6)
    echoes = scatter_about(key_of[0], (INTERVALS, RANGES, CH, 2 * PULSES), 1.0, 6.0, ((0, 4), (1, 8)))
    train_blocks = draw_train_blocks(jax.random.fold_in(key_of[5], 71), 0)
    hard_bins = with_ends((jax.random.randint(key_of[2], (INTERVALS, BINS), 0, 4) < 1).astype(jnp.int32), jax.random.fold_in(key_of[2], 1), 0, 1)
    owner_map = jax.random.permutation(key_of[3], BINS).astype(jnp.int32)
    code_phase = jnp.clip(jax.random.uniform(key_of[4], (CODE_LEN,), jnp.float32, -3.140625, 3.140625), -3.140625, 3.140625)
    return dict(echoes=echoes, train_blocks=train_blocks, hard_bins=hard_bins, owner_map=owner_map, code_phase=code_phase)


decay_rate = 0.7
diag_load = 0.1
highest = lax.Precision.HIGHEST

def doppler_table(owner_map, pulse_count):
    pulse_index = jnp.arange(pulse_count, dtype=jnp.int32)
    phase_steps = pulse_index[:, None] * owner_map[None, :] % pulse_count
    angles = phase_steps.astype(jnp.float32) * (2.0 * math.pi / pulse_count)
    cosine = jnp.cos(angles) / math.sqrt(pulse_count)
    sine_part = jnp.sin(angles) / math.sqrt(pulse_count)
    real_rows = jnp.stack([cosine, -sine_part], axis=1)
    imag_rows = jnp.stack([sine_part, cosine], axis=1)
    return jnp.concatenate([real_rows, imag_rows], axis=0).astype(jnp.bfloat16)

def doppler(samples, dft_table):
    range_count, channels, _ = samples.shape
    spectra = jnp.einsum('rcp,pkj->jrkc', samples.astype(jnp.float32), dft_table.astype(jnp.float32))
    return spectra.astype(jnp.bfloat16).reshape(dft_table.shape[2], range_count, 2 * channels)

def covariance_half(spectra, blocks, hard, block_len, easy_count):
    bin_count, range_count, row_width = spectra.shape
    channels = row_width // 2
    listed = blocks.shape[1]
    blocked = spectra.reshape(bin_count, range_count // block_len, block_len, row_width)
    chosen = jnp.take_along_axis(blocked, blocks[:, :, None, None].astype(jnp.int32), axis=1)
    keep_mask = (jnp.arange(listed, dtype=jnp.int32)[None, :] < easy_count) | (hard[:, None] == 1)
    weighted = chosen * keep_mask[:, :, None, None].astype(jnp.bfloat16)
    train_rows = chosen.reshape(bin_count, listed * block_len, row_width)
    weighted = weighted.reshape(bin_count, listed * block_len, row_width)
    real_part = train_rows[..., :channels]
    imag_part = train_rows[..., channels:]
    left_side = jnp.concatenate([train_rows, jnp.concatenate([imag_part, -real_part], axis=-1)], axis=1)
    right_side = jnp.concatenate([weighted[..., :channels], weighted[..., channels:]], axis=1)
    gram_sum = jnp.einsum('nsf,nsg->nfg', left_side.astype(jnp.float32), right_side.astype(jnp.float32))
    row_count = jnp.where(hard == 1, listed * block_len, easy_count * block_len).astype(jnp.float32)
    return gram_sum / row_count[:, None, None]

def steering(channels, beams):
    channel_index = jnp.arange(channels, dtype=jnp.int32)
    beam_index = jnp.arange(beams, dtype=jnp.int32)
    phase_steps = channel_index[:, None] * (2 * beam_index[None, :] - beams) % (2 * beams)
    angles = phase_steps.astype(jnp.float32) * (math.pi / beams)
    return (jnp.cos(angles) / math.sqrt(channels), jnp.sin(angles) / math.sqrt(channels))

def complex_product(first_re, first_im, second_re, second_im):

    def matmul(first, second):
        return jnp.einsum('nij,njk->nik', first, second, precision=highest)
    return (matmul(first_re, second_re) - matmul(first_im, second_im), matmul(first_re, second_im) + matmul(first_im, second_re))

def beam_weights(cov_half, steer_re, steer_im, steps):
    channels = cov_half.shape[2]
    identity = jnp.eye(channels, dtype=jnp.float32)
    cov_re = cov_half[:, :channels] + diag_load * identity
    cov_im = cov_half[:, channels:]
    trace_value = jnp.trace(cov_re, axis1=1, axis2=2)
    start_re = identity[None] / trace_value[:, None, None]
    start_im = jnp.zeros_like(start_re)

    def newton(step_index, inverse_pair):
        inverse_re, inverse_im = inverse_pair
        middle_re, middle_im = complex_product(cov_re, cov_im, inverse_re, inverse_im)
        return complex_product(inverse_re, inverse_im, 2.0 * identity - middle_re, -middle_im)
    inverse_re, inverse_im = lax.fori_loop(0, steps, newton, (start_re, start_im))

    def apply(matrix, table):
        return jnp.einsum('nij,jb->nib', matrix, table, precision=highest)
    vec_re = apply(inverse_re, steer_re) - apply(inverse_im, steer_im)
    vec_im = apply(inverse_re, steer_im) + apply(inverse_im, steer_re)
    beam_gain = lax.optimization_barrier(jnp.sum(steer_re * vec_re + steer_im * vec_im, axis=1))
    weight_re = vec_re / beam_gain[:, None, :]
    weight_im = vec_im / beam_gain[:, None, :]
    upper_rows = jnp.concatenate([weight_re, -weight_im], axis=2)
    lower_rows = jnp.concatenate([weight_im, weight_re], axis=2)
    return jnp.concatenate([upper_rows, lower_rows], axis=1).astype(jnp.bfloat16)

def compression_table(code_phase, block_len):
    length = code_phase.shape[0]
    input_pos = jnp.arange(2 * block_len, dtype=jnp.int32)[:, None]
    output_pos = jnp.arange(block_len, dtype=jnp.int32)[None, :]
    lag_index = input_pos - output_pos
    onehot = (lag_index[:, :, None] == jnp.arange(length, dtype=jnp.int32)[None, None, :]).astype(jnp.float32)
    code_table = jnp.stack([jnp.cos(code_phase), jnp.sin(code_phase)]) / math.sqrt(length)
    table = jnp.einsum('qpl,kl->qkp', onehot, code_table, precision=highest)
    return table.astype(jnp.bfloat16)

def compress(formed, table, block_len):
    bin_count, range_count, row_width = formed.shape
    beam_half = row_width // 2
    blocks = formed.reshape(bin_count, range_count // block_len, block_len, row_width)
    next_blocks = jnp.concatenate([blocks[:, 1:], jnp.zeros_like(blocks[:, :1])], axis=1)
    paired = jnp.concatenate([blocks, next_blocks], axis=2)
    mixed_terms = jnp.einsum('nbqe,qkp->nbkpe', paired.astype(jnp.float32), table.astype(jnp.float32))
    result_re = mixed_terms[:, :, 0, :, :beam_half] + mixed_terms[:, :, 1, :, beam_half:]
    result_im = mixed_terms[:, :, 0, :, beam_half:] - mixed_terms[:, :, 1, :, :beam_half]
    joined = jnp.concatenate([result_re, result_im], axis=-1)
    return joined.reshape(bin_count, range_count, row_width).astype(jnp.bfloat16)

def reference(echoes, train_blocks, hard_bins, owner_map, code_phase):
    dft_table = doppler_table(owner_map, PULSES)
    steer_re, steer_im = steering(CH, BEAMS)
    comp_table = compression_table(code_phase, CBLK)
    spectra_list = []
    cov_list = []
    for interval in range(INTERVALS):
        spectra = doppler(echoes[interval], dft_table)
        spectra_list.append(spectra)
        cov_list.append(covariance_half(spectra, train_blocks[interval], hard_bins[interval], RB, NTR_EASY))
    carried = jnp.zeros_like(cov_list[0])
    outputs = []
    for interval in range(INTERVALS):
        weights = beam_weights(carried, steer_re, steer_im, NS_STEPS)
        formed = jnp.einsum('nrf,nfe->nre', spectra_list[interval].astype(jnp.float32), weights.astype(jnp.float32)).astype(jnp.bfloat16)
        outputs.append(compress(formed, comp_table, CBLK))
        carried = decay_rate * carried + cov_list[interval]
    return jnp.stack(outputs)
```

```python
import functools
import math

import jax
import jax.numpy as jnp
from jax import lax
from jax.experimental import pallas as pl
from jax.experimental.pallas import tpu as pltpu
from jax.sharding import PartitionSpec as P

CH = 128
BEAMS = 128
RB = 32
NTR_EASY = 3
NS_STEPS = 12
CBLK = 128
CHUNKS = 4
GROUP = 4

decay_rate = 0.7
diag_load = 0.1
highest = lax.Precision.HIGHEST
f32 = jnp.float32
bf16 = jnp.bfloat16


def doppler_rows(owner_map, pulse_count):
    pulse_index = jnp.arange(pulse_count, dtype=jnp.int32)
    phase_steps = owner_map[:, None] * pulse_index[None, :] % pulse_count
    angles = phase_steps.astype(f32) * (2.0 * math.pi / pulse_count)
    cosine = jnp.cos(angles) / math.sqrt(pulse_count)
    sine_part = jnp.sin(angles) / math.sqrt(pulse_count)
    real_rows = jnp.concatenate([cosine, sine_part], axis=1)
    imag_rows = jnp.concatenate([-sine_part, cosine], axis=1)
    return jnp.stack([real_rows, imag_rows]).astype(bf16)


def steering(channels, beams):
    channel_index = jnp.arange(channels, dtype=jnp.int32)
    beam_index = jnp.arange(beams, dtype=jnp.int32)
    phase_steps = channel_index[:, None] * (2 * beam_index[None, :] - beams) % (2 * beams)
    angles = phase_steps.astype(f32) * (math.pi / beams)
    return (jnp.cos(angles) / math.sqrt(channels), jnp.sin(angles) / math.sqrt(channels))


def compression_rows(code_phase, block_len):
    length = code_phase.shape[0]
    input_pos = jnp.arange(2 * block_len, dtype=jnp.int32)[None, :]
    output_pos = jnp.arange(block_len, dtype=jnp.int32)[:, None]
    lag_index = input_pos - output_pos
    onehot = (lag_index[:, :, None] == jnp.arange(length, dtype=jnp.int32)[None, None, :]).astype(f32)
    code_table = jnp.stack([jnp.cos(code_phase), jnp.sin(code_phase)]) / math.sqrt(length)
    table = jnp.einsum("pql,kl->kpq", onehot, code_table, precision=highest)
    return table.reshape(2 * block_len, 2 * block_len).astype(bf16)


def doppler_kernel(x_ref, t_ref, o_ref, scr):
    rows, channels, _ = x_ref.shape
    slots = o_ref.shape[0]
    pair = 2
    for base in range(0, rows, pair):
        block = x_ref[base : base + pair].reshape(pair * channels, x_ref.shape[2])
        y = lax.dot_general(
            t_ref[...], block, (((1,), (1,)), ((), ())), preferred_element_type=f32
        )
        for i in range(pair):
            part = y[:, i * channels : (i + 1) * channels]
            scr[0, pl.ds(base + i, slots, stride=rows), :] = part[:slots]
            scr[1, pl.ds(base + i, slots, stride=rows), :] = part[slots:]
    for k in range(2):
        o_ref[:, :, k * channels : (k + 1) * channels] = (
            scr[k].reshape(slots, rows, channels).astype(bf16)
        )


def doppler(samples, table):
    ranges, channels, width = samples.shape
    slots = table.shape[0] // 2
    rows = 16
    return pl.pallas_call(
        doppler_kernel,
        grid=(ranges // rows,),
        in_specs=[
            pl.BlockSpec((rows, channels, width), lambda i: (i, 0, 0)),
            pl.BlockSpec(table.shape, lambda i: (0, 0)),
        ],
        out_specs=pl.BlockSpec((slots, rows, 2 * channels), lambda i: (0, i, 0)),
        out_shape=jax.ShapeDtypeStruct((slots, ranges, 2 * channels), bf16),
        scratch_shapes=[pltpu.VMEM((2, slots * rows, channels), f32)],
        compiler_params=pltpu.CompilerParams(vmem_limit_bytes=40 * 2**20),
        cost_estimate=pl.CostEstimate(
            flops=4 * ranges * channels * width * slots,
            bytes_accessed=2 * samples.size + 4 * slots * ranges * channels,
            transcendentals=0,
        ),
    )(samples, table)


def covariance_kernel(m_ref, s_ref, y_ref, o_ref):
    sources, group, rows, width = y_ref.shape
    ch = width // 2
    per = rows // RB
    first = pl.program_id(0) * group
    row = lax.broadcasted_iota(jnp.int32, (ch, ch), 0)
    col = lax.broadcasted_iota(jnp.int32, (ch, ch), 1)
    for g in range(group):
        y = y_ref[:, g].reshape(sources * rows, width)
        parts = []
        for b in range(sources * per):
            keep = m_ref[first + g, b]
            parts.append((y[b * RB : (b + 1) * RB].astype(f32) * keep).astype(bf16))
        masked = jnp.concatenate(parts, axis=0)
        gram = lax.dot_general(
            masked, y, (((0,), (0,)), ((), ())), preferred_element_type=f32
        )
        re = gram[:ch, :ch] + gram[ch:, ch:]
        im = gram[ch:, :ch] - gram[:ch, ch:]
        o_ref[g] = jnp.where(row <= col, re, im) * s_ref[0, first + g]


def covariance(owned, mask, scale, group):
    sources, bins, rows, width = owned.shape
    ch = width // 2
    return pl.pallas_call(
        covariance_kernel,
        grid=(bins // group,),
        in_specs=[
            pl.BlockSpec(memory_space=pltpu.SMEM),
            pl.BlockSpec(memory_space=pltpu.SMEM),
            pl.BlockSpec((sources, group, rows, width), lambda i: (0, i, 0, 0)),
        ],
        out_specs=pl.BlockSpec((group, ch, ch), lambda i: (i, 0, 0)),
        out_shape=jax.ShapeDtypeStruct((bins, ch, ch), f32),
        compiler_params=pltpu.CompilerParams(vmem_limit_bytes=40 * 2**20),
        cost_estimate=pl.CostEstimate(
            flops=2 * owned.size * width, bytes_accessed=2 * owned.size, transcendentals=0
        ),
    )(mask, scale, owned)


def split(x):
    hi = x.astype(bf16)
    return hi, (x - hi.astype(f32)).astype(bf16)


def full(half):
    ch = half.shape[1]
    re, im = half[:ch], half[ch:]
    return jnp.concatenate(
        [jnp.concatenate([re, -im], axis=1), jnp.concatenate([im, re], axis=1)], axis=0
    )


def left(half):
    hi, lo = split(half)
    return jnp.concatenate([full(hi), full(lo)], axis=0)


def right(half):
    return jnp.concatenate(split(half), axis=1)


def product(left_pair, right_pair):
    n = left_pair.shape[0] // 2
    ch = right_pair.shape[1] // 2
    p = jnp.dot(left_pair, right_pair, preferred_element_type=f32)
    return p[:n, :ch] + (p[:n, ch:] + p[n:, :ch])


def beam_kernel(terms, steps, *refs):
    cov_refs = refs[:terms]
    y_ref, sp_ref, st_ref, c_ref = refs[terms : terms + 4]
    o_ref, a_scr, x_scr = refs[-3:]
    sources, group, rows, width = y_ref.shape
    ch = width // 2
    ranges = sources * rows
    row = lax.broadcasted_iota(jnp.int32, (ch, ch), 0)
    col = lax.broadcasted_iota(jnp.int32, (ch, ch), 1)
    eye = (row == col).astype(f32)
    two_eye = jnp.concatenate([2.0 * eye, jnp.zeros_like(eye)], axis=0)
    for g in range(group):
        packed = cov_refs[0][g]
        for d in range(1, terms):
            packed = packed + (decay_rate**d) * cov_refs[d][g]
        flipped = packed.T
        re = jnp.where(row <= col, packed, flipped) + diag_load * eye
        im = jnp.where(row > col, packed, jnp.where(row < col, -flipped, 0.0))
        trace_value = jnp.sum(jnp.sum(re * eye, axis=1, keepdims=True), axis=0, keepdims=True)
        a_scr[g] = left(jnp.concatenate([re, im], axis=0))
        x_scr[g] = jnp.concatenate([eye / trace_value, jnp.zeros_like(eye)], axis=0)

    def newton(step, carry):
        held = [x_scr[g] for g in range(group)]
        middle = [two_eye - product(a_scr[g], right(held[g])) for g in range(group)]
        for g in range(group):
            x_scr[g] = product(left(held[g]), right(middle[g]))
        return carry

    lax.fori_loop(0, steps, newton, 0)
    for g in range(group):
        vec = product(left(x_scr[g]), sp_ref[...])
        gain = jnp.sum(st_ref[...] * vec, axis=0, keepdims=True)
        weights = full((vec / gain).astype(bf16))
        y = y_ref[:, g].reshape(ranges, width)
        formed = jnp.dot(y, weights, preferred_element_type=f32).astype(bf16)
        for base in range(0, ranges, CBLK):
            depth = min(2 * CBLK, ranges - base)
            mixed = jnp.dot(
                c_ref[:, :depth], formed[base : base + depth], preferred_element_type=f32
            )
            out_re = mixed[:CBLK, :ch] + mixed[CBLK:, ch:]
            out_im = mixed[:CBLK, ch:] - mixed[CBLK:, :ch]
            o_ref[g, base : base + CBLK, :] = jnp.concatenate([out_re, out_im], axis=1).astype(bf16)


def beams(covs, owned, steer_pair, steer, comp, earlier, chunk, total_bins, group):
    sources, bins, rows, width = owned.shape
    ch = width // 2
    ranges = sources * rows
    steps = bins // group
    offset = chunk * steps
    in_specs = [pl.BlockSpec((group, ch, ch), lambda i: (i, 0, 0)) for _ in covs] + [
        pl.BlockSpec((sources, group, rows, width), lambda i: (0, i, 0, 0)),
        pl.BlockSpec(steer_pair.shape, lambda i: (0, 0)),
        pl.BlockSpec(steer.shape, lambda i: (0, 0)),
        pl.BlockSpec(comp.shape, lambda i: (0, 0)),
    ]
    operands = [*covs, owned, steer_pair, steer, comp]
    aliases = {}
    if earlier is not None:
        aliases = {len(operands): 0}
        operands.append(earlier)
        in_specs.append(pl.BlockSpec(memory_space=pl.ANY))
    return pl.pallas_call(
        functools.partial(beam_kernel, len(covs), NS_STEPS),
        grid=(steps,),
        in_specs=in_specs,
        out_specs=pl.BlockSpec((None, group, ranges, width), lambda i: (0, offset + i, 0, 0)),
        out_shape=jax.ShapeDtypeStruct((1, total_bins, ranges, width), bf16),
        scratch_shapes=[
            pltpu.VMEM((group, 4 * ch, 2 * ch), bf16),
            pltpu.VMEM((group, 2 * ch, ch), f32),
        ],
        input_output_aliases=aliases,
        compiler_params=pltpu.CompilerParams(vmem_limit_bytes=48 * 2**20),
        cost_estimate=pl.CostEstimate(
            flops=bins * (2 * NS_STEPS * 2 * 4 * ch * 4 * ch * ch * 2),
            bytes_accessed=4 * owned.size,
            transcendentals=0,
        ),
    )(*operands)


def local(echoes, train_blocks, hard_bins, owner_map, code_phase):
    samples = echoes[0]
    ranges_local, channels, double_pulses = samples.shape
    owners = lax.axis_size("blk")
    segments = lax.axis_size("segment")
    blocks, hard = train_blocks[0], hard_bins[0]
    bins, listed = blocks.shape
    chunks = CHUNKS
    while bins % chunks:
        chunks //= 2
    part = bins // chunks
    group = math.gcd(part, GROUP)

    table = doppler_rows(owner_map, double_pulses // 2).reshape(
        2, owners, chunks, part, double_pulses
    )
    keep = (jnp.arange(listed, dtype=jnp.int32)[None, :] < NTR_EASY) | (hard[:, None] == 1)
    total_blocks = owners * ranges_local // RB
    mask = (
        ((blocks[:, :, None] == jnp.arange(total_blocks, dtype=jnp.int32)) & keep[:, :, None])
        .any(axis=1)
        .astype(f32)
    )
    counted = jnp.where(hard == 1, listed * RB, NTR_EASY * RB).astype(f32)
    scale = 1.0 / counted
    steer = jnp.concatenate(steering(channels, BEAMS), axis=0)
    steer_hi = lax.reduce_precision(steer, 8, 7)
    steer_pair = jnp.concatenate([steer_hi.astype(bf16), (steer - steer_hi).astype(bf16)], axis=1)
    comp = compression_rows(code_phase, CBLK)

    owned, covs = [], []
    for c in range(chunks):
        spectra = doppler(samples, table[:, :, c].reshape(2 * owners * part, double_pulses))
        spectra = spectra.reshape(owners, part, ranges_local, 2 * channels)
        owned.append(lax.all_to_all(spectra, "blk", split_axis=0, concat_axis=0, tiled=True))
    for c in range(chunks):
        span = slice(c * part, (c + 1) * part)
        own = covariance(owned[c], mask[span], scale[None, span], group)
        covs.append(
            [
                lax.ppermute(own, "segment", [(k, k + d) for k in range(segments - d)])
                for d in range(1, segments)
            ]
        )
    result = None
    for c in range(chunks):
        result = beams(covs[c], owned[c], steer_pair, steer, comp, result, c, bins, group)
    return result


def solution(mesh):
    in_specs = (
        P("segment", "blk", None, None),
        P("segment", "blk", None),
        P("segment", "blk"),
        P(),
        P(),
    )
    out_specs = P("segment", "blk", None, None)
    return jax.shard_map(local, mesh=mesh, in_specs=in_specs, out_specs=out_specs, check_vma=False)
```

```python
import functools
import math

import jax
import jax.numpy as jnp
from jax import lax
from jax.experimental import pallas as pl
from jax.experimental.pallas import tpu as pltpu
from jax.sharding import PartitionSpec as P

CH = 128
BEAMS = 128
RB = 32
NTR_EASY = 3
NS_STEPS = 12
CBLK = 128
SHARES = (3, 2, 2, 1)
GROUP = 4
SHORT_STEPS = 3

decay_rate = 0.7
diag_load = 0.1
highest = lax.Precision.HIGHEST
f32 = jnp.float32
bf16 = jnp.bfloat16


def doppler_rows(owner_map, pulse_count):
    pulse_index = jnp.arange(pulse_count, dtype=jnp.int32)
    phase_steps = owner_map[:, None] * pulse_index[None, :] % pulse_count
    angles = phase_steps.astype(f32) * (2.0 * math.pi / pulse_count)
    cosine = jnp.cos(angles) / math.sqrt(pulse_count)
    sine_part = jnp.sin(angles) / math.sqrt(pulse_count)
    real_rows = jnp.concatenate([cosine, sine_part], axis=1)
    imag_rows = jnp.concatenate([-sine_part, cosine], axis=1)
    return jnp.stack([real_rows, imag_rows]).astype(bf16)


def steering(channels, beams):
    channel_index = jnp.arange(channels, dtype=jnp.int32)
    beam_index = jnp.arange(beams, dtype=jnp.int32)
    phase_steps = channel_index[:, None] * (2 * beam_index[None, :] - beams) % (2 * beams)
    angles = phase_steps.astype(f32) * (math.pi / beams)
    return (jnp.cos(angles) / math.sqrt(channels), jnp.sin(angles) / math.sqrt(channels))


def compression_rows(code_phase, block_len):
    length = code_phase.shape[0]
    input_pos = jnp.arange(2 * block_len, dtype=jnp.int32)[None, :]
    output_pos = jnp.arange(block_len, dtype=jnp.int32)[:, None]
    lag_index = input_pos - output_pos
    onehot = (lag_index[:, :, None] == jnp.arange(length, dtype=jnp.int32)[None, None, :]).astype(f32)
    code_table = jnp.stack([jnp.cos(code_phase), jnp.sin(code_phase)]) / math.sqrt(length)
    table = jnp.einsum("pql,kl->kpq", onehot, code_table, precision=highest)
    return table.reshape(2 * block_len, 2 * block_len).astype(bf16)


def doppler_kernel(x_ref, t_ref, *refs):
    o_ref, scr = refs[-2:]
    rows, channels, _ = x_ref.shape
    slots = o_ref.shape[0]
    pair = 2
    for base in range(0, rows, pair):
        block = x_ref[base : base + pair].reshape(pair * channels, x_ref.shape[2])
        y = lax.dot_general(
            t_ref[...], block, (((1,), (1,)), ((), ())), preferred_element_type=f32
        )
        for i in range(pair):
            part = y[:, i * channels : (i + 1) * channels]
            scr[0, pl.ds(base + i, slots, stride=rows), :] = part[:slots]
            scr[1, pl.ds(base + i, slots, stride=rows), :] = part[slots:]
    for k in range(2):
        o_ref[:, :, k * channels : (k + 1) * channels] = (
            scr[k].reshape(slots, rows, channels).astype(bf16)
        )


def doppler(samples, table, after):
    ranges, channels, width = samples.shape
    slots = table.shape[0] // 2
    rows = 16
    return pl.pallas_call(
        doppler_kernel,
        grid=(ranges // rows,),
        in_specs=[
            pl.BlockSpec((rows, channels, width), lambda i: (i, 0, 0)),
            pl.BlockSpec(table.shape, lambda i: (0, 0)),
            *[pl.BlockSpec(memory_space=pl.ANY) for _ in after],
        ],
        out_specs=pl.BlockSpec((slots, rows, 2 * channels), lambda i: (0, i, 0)),
        out_shape=jax.ShapeDtypeStruct((slots, ranges, 2 * channels), bf16),
        scratch_shapes=[pltpu.VMEM((2, slots * rows, channels), f32)],
        compiler_params=pltpu.CompilerParams(vmem_limit_bytes=60 * 2**20),
        cost_estimate=pl.CostEstimate(
            flops=4 * ranges * channels * width * slots,
            bytes_accessed=2 * samples.size + 4 * slots * ranges * channels,
            transcendentals=0,
        ),
    )(samples, table, *after)


def covariance_kernel(m_ref, s_ref, y_ref, o_ref):
    sources, group, rows, width = y_ref.shape
    ch = width // 2
    per = rows // RB
    first = pl.program_id(0) * group
    row = lax.broadcasted_iota(jnp.int32, (ch, ch), 0)
    col = lax.broadcasted_iota(jnp.int32, (ch, ch), 1)
    for g in range(group):
        y = y_ref[:, g].reshape(sources * rows, width)
        parts = []
        for b in range(sources * per):
            keep = m_ref[first + g, b]
            parts.append((y[b * RB : (b + 1) * RB].astype(f32) * keep).astype(bf16))
        masked = jnp.concatenate(parts, axis=0)
        gram = lax.dot_general(
            masked, y, (((0,), (0,)), ((), ())), preferred_element_type=f32
        )
        re = gram[:ch, :ch] + gram[ch:, ch:]
        im = gram[ch:, :ch] - gram[:ch, ch:]
        o_ref[g] = jnp.where(row <= col, re, im) * s_ref[0, first + g]


def covariance(owned, mask, scale, group):
    sources, bins, rows, width = owned.shape
    ch = width // 2
    return pl.pallas_call(
        covariance_kernel,
        grid=(bins // group,),
        in_specs=[
            pl.BlockSpec(memory_space=pltpu.SMEM),
            pl.BlockSpec(memory_space=pltpu.SMEM),
            pl.BlockSpec((sources, group, rows, width), lambda i: (0, i, 0, 0)),
        ],
        out_specs=pl.BlockSpec((group, ch, ch), lambda i: (i, 0, 0)),
        out_shape=jax.ShapeDtypeStruct((bins, ch, ch), f32),
        compiler_params=pltpu.CompilerParams(vmem_limit_bytes=40 * 2**20),
        cost_estimate=pl.CostEstimate(
            flops=2 * owned.size * width, bytes_accessed=2 * owned.size, transcendentals=0
        ),
    )(mask, scale, owned)


def split(x):
    hi = x.astype(bf16)
    return hi, (x - hi.astype(f32)).astype(bf16)


def full(half):
    ch = half.shape[1]
    re, im = half[:ch], half[ch:]
    return jnp.concatenate(
        [jnp.concatenate([re, -im], axis=1), jnp.concatenate([im, re], axis=1)], axis=0
    )


def left(half):
    hi, lo = split(half)
    return jnp.concatenate([full(hi), full(lo)], axis=0)


def right(half):
    return jnp.concatenate(split(half), axis=1)


def product(left_pair, right_pair):
    n = right_pair.shape[0]
    ch = right_pair.shape[1] // 2
    p = jnp.dot(left_pair, right_pair, preferred_element_type=f32)
    total = p[:n, :ch] + p[:n, ch:]
    return total if left_pair.shape[0] == n else total + p[n:, :ch]


def beam_kernel(terms, steps, *refs):
    cov_refs = refs[:terms]
    y_ref, sp_ref, st_ref, c_ref = refs[terms : terms + 4]
    o_ref, done_ref, a_scr, x_scr = refs[-4:]
    done_ref[...] = jnp.zeros_like(done_ref)
    sources, group, rows, width = y_ref.shape
    ch = width // 2
    ranges = sources * rows
    row = lax.broadcasted_iota(jnp.int32, (ch, ch), 0)
    col = lax.broadcasted_iota(jnp.int32, (ch, ch), 1)
    eye = (row == col).astype(f32)
    for g in range(group):
        packed = cov_refs[0][g]
        for d in range(1, terms):
            packed = packed + (decay_rate**d) * cov_refs[d][g]
        flipped = packed.T
        re = jnp.where(row <= col, packed, flipped) + diag_load * eye
        im = jnp.where(row > col, packed, jnp.where(row < col, -flipped, 0.0))
        trace_value = jnp.sum(jnp.sum(re * eye, axis=1, keepdims=True), axis=0, keepdims=True)
        a_scr[g] = left(jnp.concatenate([re, im], axis=0))
        x_scr[g] = jnp.concatenate([2.0 * eye - re / trace_value, -im / trace_value], axis=0) / trace_value

    def newton(depth, step, carry):
        held = [x_scr[g] for g in range(group)]
        pairs = [right(x) for x in held]
        middle = [product(a_scr[g, :depth], pairs[g]) for g in range(group)]
        for g in range(group):
            x_scr[g] = 2.0 * held[g] - product(full(pairs[g][:, :ch]), right(middle[g]))
        return carry

    short = min(SHORT_STEPS, steps - 1)
    lax.fori_loop(0, short, functools.partial(newton, 2 * ch), 0)
    lax.fori_loop(short, steps - 1, functools.partial(newton, 4 * ch), 0)
    for g in range(group):
        vec = product(left(x_scr[g]), sp_ref[...])
        gain = jnp.sum(st_ref[...] * vec, axis=0, keepdims=True)
        weights = full((vec / gain).astype(bf16))
        y = y_ref[:, g].reshape(ranges, width)
        formed = jnp.dot(y, weights, preferred_element_type=f32).astype(bf16)
        for base in range(0, ranges, CBLK):
            depth = min(2 * CBLK, ranges - base)
            mixed = jnp.dot(
                c_ref[:, :depth], formed[base : base + depth], preferred_element_type=f32
            )
            out_re = mixed[:CBLK, :ch] + mixed[CBLK:, ch:]
            out_im = mixed[:CBLK, ch:] - mixed[CBLK:, :ch]
            o_ref[g, base : base + CBLK, :] = jnp.concatenate([out_re, out_im], axis=1).astype(bf16)


def beams(covs, owned, steer_pair, steer, comp, earlier, start, total_bins, group):
    sources, bins, rows, width = owned.shape
    ch = width // 2
    ranges = sources * rows
    steps = bins // group
    offset = start // group
    in_specs = [pl.BlockSpec((group, ch, ch), lambda i: (i, 0, 0)) for _ in covs] + [
        pl.BlockSpec((sources, group, rows, width), lambda i: (0, i, 0, 0)),
        pl.BlockSpec(steer_pair.shape, lambda i: (0, 0)),
        pl.BlockSpec(steer.shape, lambda i: (0, 0)),
        pl.BlockSpec(comp.shape, lambda i: (0, 0)),
    ]
    operands = [*covs, owned, steer_pair, steer, comp]
    aliases = {}
    if earlier is not None:
        aliases = {len(operands): 0}
        operands.append(earlier)
        in_specs.append(pl.BlockSpec(memory_space=pl.ANY))
    return pl.pallas_call(
        functools.partial(beam_kernel, len(covs), NS_STEPS),
        grid=(steps,),
        in_specs=in_specs,
        out_specs=[
            pl.BlockSpec((None, group, ranges, width), lambda i: (0, offset + i, 0, 0)),
            pl.BlockSpec((8, 128), lambda i: (0, 0)),
        ],
        out_shape=[
            jax.ShapeDtypeStruct((1, total_bins, ranges, width), bf16),
            jax.ShapeDtypeStruct((8, 128), f32),
        ],
        scratch_shapes=[
            pltpu.VMEM((group, 4 * ch, 2 * ch), bf16),
            pltpu.VMEM((group, 2 * ch, ch), f32),
        ],
        input_output_aliases=aliases,
        compiler_params=pltpu.CompilerParams(vmem_limit_bytes=48 * 2**20),
        cost_estimate=pl.CostEstimate(
            flops=bins * (3 * NS_STEPS * 4 * ch * 4 * ch * ch),
            bytes_accessed=4 * owned.size,
            transcendentals=0,
        ),
    )(*operands)


def local(echoes, train_blocks, hard_bins, owner_map, code_phase):
    samples = echoes[0]
    ranges_local, channels, double_pulses = samples.shape
    owners = lax.axis_size("blk")
    segments = lax.axis_size("segment")
    blocks, hard = train_blocks[0], hard_bins[0]
    bins, listed = blocks.shape
    unit = bins // sum(SHARES)
    shares = [unit * share for share in SHARES]
    shares[-1] += bins - sum(shares)
    shares = [share for share in shares if share > 0]
    starts = [sum(shares[:c]) for c in range(len(shares))]
    chunks = len(shares)

    table = doppler_rows(owner_map, double_pulses // 2).reshape(
        2, owners, bins, double_pulses
    )
    keep = (jnp.arange(listed, dtype=jnp.int32)[None, :] < NTR_EASY) | (hard[:, None] == 1)
    total_blocks = owners * ranges_local // RB
    mask = (
        ((blocks[:, :, None] == jnp.arange(total_blocks, dtype=jnp.int32)) & keep[:, :, None])
        .any(axis=1)
        .astype(f32)
    )
    counted = jnp.where(hard == 1, listed * RB, NTR_EASY * RB).astype(f32)
    scale = 1.0 / counted
    steer = jnp.concatenate(steering(channels, BEAMS), axis=0)
    steer_hi = lax.reduce_precision(steer, 8, 7)
    steer_pair = jnp.concatenate([steer_hi.astype(bf16), (steer - steer_hi).astype(bf16)], axis=1)
    comp = compression_rows(code_phase, CBLK)

    groups = [math.gcd(math.gcd(share, GROUP), start) for share, start in zip(shares, starts)]
    owned, covs = [], []
    result = None

    def send(c, after):
        span = slice(starts[c], starts[c] + shares[c])
        rows = table[:, :, span].reshape(2 * owners * shares[c], double_pulses)
        spectra = doppler(samples, rows, after)
        spectra = spectra.reshape(owners, shares[c], ranges_local, 2 * channels)
        owned.append(lax.all_to_all(spectra, "blk", split_axis=0, concat_axis=0, tiled=True))
        return spectra

    def exchange(c):
        span = slice(starts[c], starts[c] + shares[c])
        own = covariance(owned[c], mask[span], scale[None, span], groups[c])
        covs.append(
            [
                lax.ppermute(own, "segment", [(k, k + d) for k in range(segments - d)])
                for d in range(1, segments)
            ]
        )
        return covs[c]

    def form(c, earlier):
        return beams(
            covs[c], owned[c], steer_pair, steer, comp, earlier, starts[c], bins, groups[c]
        )

    first = send(0, ())
    if chunks > 1:
        send(1, [first])
    for c in range(chunks):
        after = [*exchange(c)]
        if c > 0:
            result, done = form(c - 1, result)
            after.append(done)
        if c + 2 < chunks:
            send(c + 2, after)
    result, _ = form(chunks - 1, result)
    return result


def solution(mesh):
    in_specs = (
        P("segment", "blk", None, None),
        P("segment", "blk", None),
        P("segment", "blk"),
        P(),
        P(),
    )
    out_specs = P("segment", "blk", None, None)
    return jax.shard_map(local, mesh=mesh, in_specs=in_specs, out_specs=out_specs, check_vma=False)
```
